32 devices in a mesh: fsdp: 16 (over z, y, x), basis: 2 (over core).
Axes of the slice: x: 2, y: 2, z: 4, core: 2. Of those that a mesh axis runs over, the one named last changes fastest.
Arguments:
- gradient: bfloat16 [2, 576, 18432], P('basis', 'fsdp'), may hold values from -6000 to 6000
- first_moment: bfloat16 [2, 576, 18432], P('basis', 'fsdp'), may hold values from -0.29882812 to 0.29882812
- second_moment: bfloat16 [2, 576, 18432], P('basis', None, 'fsdp'), may hold values from 0.0099487305 to 0.5
- statistic: float32 [2, 576, 576], P('basis', 'fsdp'), may hold values from -1 to 3, as said below
- eigenbasis: float32 [2, 576, 576], P('basis', 'fsdp'), may hold values from -1 to 2, as said below
Outputs:
- update: bfloat16 [2, 576, 18432], P('basis', 'fsdp')
- new_first: bfloat16 [2, 576, 18432], P('basis', 'fsdp')
- new_second: bfloat16 [2, 576, 18432], P('basis', None, 'fsdp')
- new_stat: float32 [2, 576, 576], P('basis', 'fsdp')
- new_basis: float32 [2, 576, 576], P('basis', 'fsdp')
The draws below stay inside these ranges and needn't reach their ends.
Inputs may be any that keep to these rules, and one draw needn't show every extreme that they name: `statistic`: symmetric in each block, positive definite. `eigenbasis`: each block invertible.
All inputs are finite; a program needn't handle non-finite values.
Results may differ from the reference program's by a relative error of at most 0.00055.
The reference program's roundings to bfloat16 on the way (of `rounded_basis` and `direction`) count: a program that leaves them out, or rounds other values in their place, can miss the bound.
Values may be sent and summed in bfloat16 or wider, within the bound.
A program may use at most 128 MiB of HBM per device.

```python
import math
import jax
import jax.numpy as jnp
from jax import lax

FF = 18432
BK = 576
NBLK = 2


def draw_gradient(key, part):
    key = jax.random.fold_in(key, 11)
    key_base, key_rows, key_cols = jax.random.split(key, 3)
    position = jnp.arange(BK, dtype=jnp.float32) / BK
    rising = (1.0 + 2.0 * position)[None, :, None]
    row_scale = jnp.exp(jax.random.uniform(key_rows, (NBLK, BK, 1), jnp.float32, 0.0, math.log(10.0)))
    col_scale = jnp.exp(jax.random.uniform(key_cols, (NBLK, 1, FF), jnp.float32, 0.0, math.log(10.0)))
    base = jnp.clip(jax.random.normal(key_base, (NBLK, BK, FF), jnp.float32), -5.0, 5.0)
    return (base * row_scale * col_scale * rising).astype(jnp.bfloat16)


def draw_statistic(key, part):
    key = jax.random.fold_in(key, 23)
    key_noise, key_diag = jax.random.split(key, 2)
    noise = jnp.clip(jax.random.normal(key_noise, (NBLK, BK, BK), jnp.float32), -5.0, 5.0) * (0.15 / math.sqrt(BK))
    symmetric = (noise + jnp.swapaxes(noise, 1, 2)) * 0.7071
    diagonal = jnp.exp(jax.random.uniform(key_diag, (NBLK, BK), jnp.float32, math.log(0.5), math.log(2.0)))
    return symmetric + diagonal[:, :, None] * jnp.eye(BK, dtype=jnp.float32)[None]


def draw_eigenbasis(key, part):
    key = jax.random.fold_in(key, 37)
    noise = jnp.clip(jax.random.normal(key, (NBLK, BK, BK), jnp.float32), -5.0, 5.0) * (0.3 / math.sqrt(BK))
    return noise + jnp.eye(BK, dtype=jnp.float32)[None]


def levels(rng, shape, shards, smallest, largest):
    def one(axis_at, shards_of):
        heights = jax.random.uniform(jax.random.fold_in(jax.random.fold_in(rng, 6), axis_at), (shards_of,), jnp.float32, smallest / len(shards), largest / len(shards))
        return jnp.repeat(jnp.exp(heights), shape[axis_at] // shards_of).reshape((-1,) + (1,) * (len(shape) - axis_at - 1))

    loudness = one(*shards[0])
    for cut in shards[1:]:
        loudness = loudness * one(*cut)
    return loudness


def normal_values(key, extent, scale, limit, cuts=(), held_as=jnp.bfloat16):
    values = scale * jax.random.normal(key, extent, jnp.float32)
    if cuts:
        values = values * levels(key, extent, cuts, -0.22, 0.18)
    return jnp.clip(values, -limit, limit).astype(held_as)


def setup_inputs(seed: int = 0) -> dict:
    key_of = jax.random.split(jax.random.key(seed), 6)
    return {
        "gradient": draw_gradient(jax.random.fold_in(key_of[5], 71), 0),
        "first_moment": normal_values(key_of[1], (NBLK, BK, FF), 0.05, 0.29882812, ((0, 2), (1, 16))),
        "second_moment": jnp.clip(jnp.exp(math.log(0.5) - 3.9171631 * jax.random.uniform(key_of[2], (NBLK, BK, FF), jnp.float32) ** levels(key_of[2], (NBLK, BK, FF), ((0, 2), (2, 16)), -0.2, 0.2)), 0.0099487305, 0.5).astype(jnp.bfloat16),
        "statistic": draw_statistic(jax.random.fold_in(key_of[5], 71), 0),
        "eigenbasis": draw_eigenbasis(jax.random.fold_in(key_of[5], 71), 0),
    }


beta_first = 0.9
beta_second = 0.95
clip_rms = 0.5
tiny_eps = 1e-08

def reference(gradient, first_moment, second_moment, statistic, eigenbasis):
    sums = lax.map(lambda block: jnp.sum(jnp.square(block.astype(jnp.float32))), gradient)
    entries = NBLK * BK * FF
    clip_factor = jnp.minimum(1.0, clip_rms / jnp.sqrt(jnp.sum(sums) / entries + 1e-06))

    def one_block(items):
        grad_block, moment_block, second_block, stat_block, basis_block = items
        rounded_basis = basis_block.astype(jnp.bfloat16)
        grad_rot = jnp.dot(rounded_basis.T.astype(jnp.float32), grad_block.astype(jnp.float32), preferred_element_type=jnp.float32)
        moment_rot = jnp.dot(rounded_basis.T.astype(jnp.float32), moment_block.astype(jnp.float32), preferred_element_type=jnp.float32)
        scaled_rot = clip_factor * grad_rot
        rotated_first = beta_first * moment_rot + (1.0 - beta_first) * scaled_rot
        second_full = beta_second * second_block.astype(jnp.float32) + (1.0 - beta_second) * scaled_rot * scaled_rot
        direction = (rotated_first / (jnp.sqrt(second_full) + tiny_eps)).astype(jnp.bfloat16)
        update = jnp.dot(rounded_basis.astype(jnp.float32), direction.astype(jnp.float32), preferred_element_type=jnp.float32).astype(jnp.bfloat16)
        new_first = (beta_first * moment_block.astype(jnp.float32) + (1.0 - beta_first) * clip_factor * grad_block.astype(jnp.float32)).astype(jnp.bfloat16)
        covariance = jnp.dot(grad_block.astype(jnp.float32), grad_block.T.astype(jnp.float32), preferred_element_type=jnp.float32) / FF
        new_stat = beta_second * stat_block + (1.0 - beta_second) * clip_factor * clip_factor * covariance
        refreshed = jnp.dot(new_stat, basis_block, precision=lax.Precision.HIGHEST)
        gram_matrix = jnp.dot(refreshed.T, refreshed, precision=lax.Precision.HIGHEST)
        factor = jnp.linalg.cholesky(gram_matrix)
        new_basis = lax.linalg.triangular_solve(factor, refreshed, left_side=False, lower=True, transpose_a=True)
        return (update, new_first, second_full.astype(jnp.bfloat16), new_stat, new_basis)
    update, new_first, new_second, new_stat, new_basis = lax.map(one_block, (gradient, first_moment, second_moment, statistic, eigenbasis))
    return (update, new_first, new_second, new_stat, new_basis)
```

```python
import functools

import jax
import jax.numpy as jnp
import numpy as np
from jax import lax
from jax.experimental import pallas as pl
from jax.experimental.pallas import tpu as pltpu
from jax.sharding import PartitionSpec as P

beta_first = 0.9
beta_second = 0.95
clip_rms = 0.5
tiny_eps = 1e-08
NB = 128
MESH = pl.DeviceIdType.MESH
HI = lax.Precision.HIGHEST
F32 = jnp.float32
BF16 = jnp.bfloat16


def dot(left, right, dims, precision=None):
    return lax.dot_general(
        left, right, (dims, ((), ())), preferred_element_type=F32, precision=precision
    )


def inverse_factor(tiles):
    lane = lax.broadcasted_iota(jnp.int32, (8, NB), 1)
    row = lax.broadcasted_iota(jnp.int32, (8, NB), 0)
    count = NB // 8
    for j in range(NB):
        home, sub = divmod(j, 8)
        pivot_row = tiles[home][sub : sub + 1, :]
        inverse = 1.0 / pivot_row[:, j : j + 1]
        at_j = lane == j
        scaled = jnp.where(at_j[:1], 1.0, pivot_row) * inverse
        for t in range(home, count):
            column = tiles[t][:, j : j + 1]
            updated = jnp.where(at_j, 0.0, tiles[t]) - column * scaled
            tiles[t] = jnp.where(row > sub, updated, tiles[t]) if t == home else updated
    out = []
    for t in range(count):
        on_diag = lane == row + 8 * t
        pivot = jnp.sum(jnp.where(on_diag, tiles[t], 0.0), axis=1, keepdims=True)
        unit = jnp.where(on_diag, 1.0, jnp.where(lane < row + 8 * t, tiles[t], 0.0))
        out.append(unit * lax.rsqrt(pivot))
    return jnp.concatenate(out, axis=0)


def kernel(
    n, nb, entries, cols, bk, split,
    g_ref, m_ref, v_ref, st_ref, eb_ref, pm_ref,
    upd_ref, nf_ref, ns_ref, nst_ref, q_ref,
    gs, ms, us, gr, bs, bb, covs, rs, ss, gc, rf, af, ro, sums_a, sums_b, lin,
    g_s, g_r, m_s, m_r, u_s, u_r, b_s, b_r, c_s, c_r, a_s, a_r, x_s, x_r, y_s, y_r, own_sem,
):
    me = lax.axis_index("fsdp")
    core = lax.axis_index("basis")
    rp = gs.shape[1]
    rf_rows = bs.shape[1]
    kp = bs.shape[2]
    total = n * cols
    width = 384 if cols % 384 == 0 else cols
    fold = 8 * 128

    def chunk(ref, d):
        if split:
            return ref.at[d]
        return ref.at[:, pl.ds(pl.multiple_of(d * cols, 128), cols)]

    def peers(fn):
        def body(k, carry):
            fn(lax.rem(me + k, n))
            return carry
        lax.fori_loop(1, n, body, 0)

    def send(source_of, target, s_sem, r_sem):
        def one(d):
            pltpu.make_async_remote_copy(
                src_ref=source_of(d), dst_ref=target(me), send_sem=s_sem.at[d],
                recv_sem=r_sem.at[me], device_id={"fsdp": d}, device_id_type=MESH,
            ).start()
        peers(one)

    def wait_recv(source_of, target, s_sem, r_sem):
        def one(d):
            pltpu.make_async_remote_copy(
                src_ref=source_of(d), dst_ref=target(d), send_sem=s_sem.at[d],
                recv_sem=r_sem.at[d], device_id={"fsdp": d}, device_id_type=MESH,
            ).wait_recv()
        peers(one)

    def wait_send(source_of, target, s_sem, r_sem):
        def one(d):
            pltpu.make_async_remote_copy(
                src_ref=source_of(d), dst_ref=target(me), send_sem=s_sem.at[d],
                recv_sem=r_sem.at[me], device_id={"fsdp": d}, device_id_type=MESH,
            ).wait_send()
        peers(one)

    grads = (lambda d: chunk(g_ref, d), lambda s: gs.at[s], g_s, g_r)
    moments = (lambda d: chunk(m_ref, d), lambda s: ms.at[s], m_s, m_r)
    updates = (lambda d: us.at[d], lambda s: chunk(upd_ref, s), u_s, u_r)
    bases = (lambda d: eb_ref, lambda s: bs.at[s], b_s, b_r)
    shares = (lambda d: covs.at[d], lambda s: rs.at[s], c_s, c_r)
    stats = (lambda d: nst_ref, lambda s: ss.at[s], a_s, a_r)
    squares = (lambda d: sums_a.at[n], lambda s: sums_a.at[s], x_s, x_r)

    barrier = pltpu.get_barrier_semaphore()

    def greet(d):
        pl.semaphore_signal(barrier, inc=1, device_id={"fsdp": d}, device_id_type=MESH)

    peers(greet)
    for k in range(1, nb):
        pl.semaphore_signal(
            barrier, inc=1, device_id={"basis": lax.rem(core + k, nb)}, device_id_type=MESH
        )
    pl.semaphore_wait(barrier, n - 1 + nb - 1)

    send(*grads)
    send(*bases)
    own = [
        pltpu.make_async_copy(chunk(g_ref, me), gs.at[me], own_sem.at[0]),
        pltpu.make_async_copy(chunk(m_ref, me), ms.at[me], own_sem.at[1]),
        pltpu.make_async_copy(eb_ref, bs.at[me], own_sem.at[2]),
    ]
    for copy in own:
        copy.start()

    def add_squares(d, acc):
        v = chunk(g_ref, d)[...].astype(F32)
        return acc + jnp.sum(v * v, axis=0, keepdims=True)

    acc = lax.fori_loop(0, n, add_squares, jnp.zeros((1, cols), F32))
    sums_a[n] = jnp.full((8, 128), jnp.sum(acc), F32)
    send(*squares)
    sums_a[me] = sums_a[n]
    wait_recv(*squares)
    sums_b[nb] = jnp.sum(sums_a[0:n], axis=0)
    sums_b[core] = sums_b[nb]

    def cross(k):
        other = lax.rem(core + k, nb)
        return pltpu.make_async_remote_copy(
            src_ref=sums_b.at[nb], dst_ref=sums_b.at[core], send_sem=y_s.at[other],
            recv_sem=y_r.at[core], device_id={"basis": other}, device_id_type=MESH,
        )

    def cross_recv(k):
        other = lax.rem(core + k, nb)
        return pltpu.make_async_remote_copy(
            src_ref=sums_b.at[nb], dst_ref=sums_b.at[other], send_sem=y_s.at[other],
            recv_sem=y_r.at[other], device_id={"basis": other}, device_id_type=MESH,
        )

    for k in range(1, nb):
        cross(k).start()

    for copy in own:
        copy.wait()
    wait_recv(*grads)
    gc[...] = dot(pm_ref[...], gs[...].reshape(n * rp, cols), ((1,), (0,))).astype(BF16)

    def share(s, carry):
        covs[s] = dot(gs[s], gc[...], ((1,), (1,)))[:rf_rows]
        return carry

    lax.fori_loop(0, n, share, 0)
    send(*shares)

    for k in range(1, nb):
        cross_recv(k).wait_recv()
    mean = jnp.sum(sums_b[0:nb], axis=0)[0:1, 0:1] / entries
    clip = jnp.minimum(1.0, clip_rms / jnp.sqrt(mean + 1e-06))

    def first(d, carry):
        chunk(nf_ref, d)[...] = (
            beta_first * chunk(m_ref, d)[...].astype(F32)
            + (1.0 - beta_first) * clip * chunk(g_ref, d)[...].astype(F32)
        ).astype(BF16)
        return carry

    lax.fori_loop(0, n, first, 0)

    wait_recv(*bases)

    def narrow(s, carry):
        v = bs[s]
        if rp > rf_rows:
            v = jnp.concatenate([v, jnp.zeros((rp - rf_rows, kp), F32)], axis=0)
        bb[s] = v.astype(BF16)
        return carry

    lax.fori_loop(0, n, narrow, 0)

    def columns(i):
        if cols == width:
            return pl.ds(0, cols)
        return pl.ds(pl.multiple_of(i * width, 128), width)

    def rotate(i, carry):
        at = columns(i)
        basis = bb[...].reshape(n * rp, kp)[:, :bk]
        rot = clip * dot(basis, gs[:, :, at].reshape(n * rp, width), ((0,), (0,)))
        gr[:, at] = rot
        ns_ref[:, at] = (
            beta_second * v_ref[:, at].astype(F32) + (1.0 - beta_second) * rot * rot
        ).astype(BF16)
        return carry

    lax.fori_loop(0, cols // width, rotate, 0)

    wait_recv(*shares)
    rs[me] = covs[me]

    def add_share(s, acc):
        return acc + rs[s]

    cov = lax.fori_loop(0, n, add_share, jnp.zeros((rf_rows, kp), F32)) / total
    nst_ref[...] = beta_second * st_ref[...] + (1.0 - beta_second) * clip * clip * cov
    send(*stats)
    send(*moments)
    ss[me] = nst_ref[...]
    wait_recv(*stats)

    def refresh(i, carry):
        at = pl.ds(pl.multiple_of(i * NB, NB), NB)
        rf[at, :] = dot(
            ss[:, :, at].reshape(n * rf_rows, NB), bs[...].reshape(n * rf_rows, kp),
            ((0,), (0,)), HI,
        )
        return carry

    lax.fori_loop(0, kp // NB, refresh, 0)
    rows = bk // n
    r_at = lax.broadcasted_iota(jnp.int32, (rf_rows, kp), 0)
    c_at = lax.broadcasted_iota(jnp.int32, (rf_rows, kp), 1)
    pick = jnp.where((c_at == r_at + me * rows) & (r_at < rows), 1.0, 0.0).astype(F32)
    ro[...] = dot(pick, rf[...], ((1,), (0,)), HI)

    def gram(i, carry):
        at = pl.ds(pl.multiple_of(i * NB, NB), NB)
        part = dot(rf[:, at], rf[...], ((0,), (0,)), HI)
        r = lax.broadcasted_iota(jnp.int32, (NB, kp), 0) + i * NB
        c = lax.broadcasted_iota(jnp.int32, (NB, kp), 1)
        af[at, :] = part + jnp.where((r == c) & (r >= bk), 1.0, 0.0)
        return carry

    lax.fori_loop(0, kp // NB, gram, 0)

    def precondition():
        wait_recv(*moments)

        def body(i, carry):
            at = columns(i)
            basis = bb[...].reshape(n * rp, kp)[:, :bk]
            rot = gr[:, at]
            moment = dot(basis, ms[:, :, at].reshape(n * rp, width), ((0,), (0,)))
            second = beta_second * v_ref[:, at].astype(F32) + (1.0 - beta_second) * rot * rot
            direction = (
                (beta_first * moment + (1.0 - beta_first) * rot) / (jnp.sqrt(second) + tiny_eps)
            ).astype(BF16)
            us[:, :, at] = (
                dot(basis, direction, ((1,), (0,))).astype(BF16).reshape(n, rp, width)
            )
            return carry

        lax.fori_loop(0, cols // width, body, 0)
        send(*updates)
        chunk(upd_ref, me)[...] = us[me]

    blocks = kp // NB

    def eliminate(b, carry):
        @pl.when(b == blocks // 2)
        def _():
            precondition()

        at = pl.ds(pl.multiple_of(b * NB, NB), NB)
        tiles = [
            af[pl.ds(pl.multiple_of(b * NB + 8 * t, 8), 8), at] for t in range(NB // 8)
        ]
        lin[...] = inverse_factor(tiles)
        panel = dot(lin[...], af[at, :], ((1,), (0,)), HI)
        q = dot(ro[:, at], lin[...], ((1,), (1,)), HI)
        q_ref[:, at] = q
        ro[...] = ro[...] - dot(q, panel, ((1,), (0,)), HI)
        af[...] = af[...] - dot(panel, panel, ((0,), (0,)), HI)
        return carry

    lax.fori_loop(0, blocks, eliminate, 0)

    wait_recv(*updates)
    for k in range(1, nb):
        cross(k).wait_send()
    for phase in (grads, bases, squares, shares, stats, moments, updates):
        wait_send(*phase)


def ceil_to(value, step):
    return -(-value // step) * step


def local(n, nb, gradient, first_moment, second_moment, statistic, eigenbasis):
    rows, ff = gradient.shape[1:]
    bk = rows * n
    cols = ff // n
    rp = ceil_to(rows, 16)
    rf_rows = ceil_to(rows, 8)
    kp = ceil_to(bk, NB)
    split = cols % 128 != 0

    def wide(x):
        x = jnp.pad(x[0], ((0, rp - rows), (0, 0)))
        if split:
            x = jnp.swapaxes(x.reshape(rp, n, cols), 0, 1)
        return x

    def narrow(x):
        if split:
            x = jnp.swapaxes(x, 0, 1).reshape(rp, ff)
        return x[None, :rows]

    def square(x):
        return jnp.pad(x[0], ((0, rf_rows - rows), (0, kp - bk)))

    pick = np.zeros((kp, n * rp), np.float32)
    at = np.arange(bk)
    pick[at, (at // rows) * rp + at % rows] = 1.0
    big = (n, rp, cols) if split else (rp, ff)
    vmem = pl.BlockSpec(memory_space=pltpu.VMEM)
    dma = pltpu.SemaphoreType.DMA
    upd, nf, ns, nst, q = pl.pallas_call(
        functools.partial(kernel, n, nb, nb * bk * ff, cols, bk, split),
        out_shape=(
            jax.ShapeDtypeStruct(big, BF16),
            jax.ShapeDtypeStruct(big, BF16),
            jax.ShapeDtypeStruct((bk, cols), BF16),
            jax.ShapeDtypeStruct((rf_rows, kp), F32),
            jax.ShapeDtypeStruct((rf_rows, kp), F32),
        ),
        in_specs=[vmem] * 6,
        out_specs=(vmem,) * 5,
        scratch_shapes=[
            pltpu.VMEM((n, rp, cols), BF16),
            pltpu.VMEM((n, rp, cols), BF16),
            pltpu.VMEM((n, rp, cols), BF16),
            pltpu.VMEM((bk, cols), F32),
            pltpu.VMEM((n, rf_rows, kp), F32),
            pltpu.VMEM((n, rp, kp), BF16),
            pltpu.VMEM((n, rf_rows, kp), F32),
            pltpu.VMEM((n, rf_rows, kp), F32),
            pltpu.VMEM((n, rf_rows, kp), F32),
            pltpu.VMEM((kp, cols), BF16),
            pltpu.VMEM((kp, kp), F32),
            pltpu.VMEM((kp, kp), F32),
            pltpu.VMEM((rf_rows, kp), F32),
            pltpu.VMEM((n + 1, 8, 128), F32),
            pltpu.VMEM((nb + 1, 8, 128), F32),
            pltpu.VMEM((NB, NB), F32),
        ]
        + [dma((n,))] * 14
        + [dma((nb,))] * 2
        + [dma((3,))],
        compiler_params=pltpu.CompilerParams(
            collective_id=0, has_side_effects=True, vmem_limit_bytes=56 * 1024 * 1024
        ),
    )(
        wide(gradient),
        wide(first_moment),
        second_moment[0],
        square(statistic),
        square(eigenbasis),
        jnp.asarray(pick, BF16),
    )
    return (narrow(upd), narrow(nf), ns[None], nst[None, :rows, :bk], q[None, :rows, :bk])


def solution(mesh):
    n, nb = mesh.shape["fsdp"], mesh.shape["basis"]
    rows = P("basis", "fsdp", None)
    columns = P("basis", None, "fsdp")
    return jax.shard_map(
        functools.partial(local, n, nb),
        mesh=mesh,
        in_specs=(rows, rows, columns, rows, rows),
        out_specs=(rows, rows, columns, rows, rows),
        check_vma=False,
    )
```

```python
import functools

import jax
import jax.numpy as jnp
import numpy as np
from jax import lax
from jax.experimental import pallas as pl
from jax.experimental.pallas import tpu as pltpu
from jax.sharding import PartitionSpec as P

beta_first = 0.9
beta_second = 0.95
clip_rms = 0.5
tiny_eps = 1e-08
NB = 128
MESH = pl.DeviceIdType.MESH
HI = lax.Precision.HIGHEST
F32 = jnp.float32
BF16 = jnp.bfloat16


def dot(left, right, dims, precision=None):
    return lax.dot_general(
        left, right, (dims, ((), ())), preferred_element_type=F32, precision=precision
    )


def inverse_factor(tiles, steps):
    lane = lax.broadcasted_iota(jnp.int32, (8, NB), 1)
    row = lax.broadcasted_iota(jnp.int32, (8, NB), 0)
    count = NB // 8
    active = -(-steps // 8)
    for j in range(steps):
        home, sub = divmod(j, 8)
        pivot_row = tiles[home][sub : sub + 1, :]
        inverse = 1.0 / pivot_row[:, j : j + 1]
        at_j = lane == j
        scaled = jnp.where(at_j[:1], 1.0, pivot_row) * inverse
        for t in range(home, active):
            column = tiles[t][:, j : j + 1]
            updated = jnp.where(at_j, 0.0, tiles[t]) - column * scaled
            tiles[t] = jnp.where(row > sub, updated, tiles[t]) if t == home else updated
    out = []
    for t in range(count):
        on_diag = lane == row + 8 * t
        pivot = jnp.sum(jnp.where(on_diag, tiles[t], 0.0), axis=1, keepdims=True)
        unit = jnp.where(on_diag, 1.0, jnp.where(lane < row + 8 * t, tiles[t], 0.0))
        out.append(unit * lax.rsqrt(pivot))
    return jnp.concatenate(out, axis=0)


def kernel(
    n, nb, entries, cols, bk, split,
    g_ref, m_ref, v_ref, st_ref, eb_ref, pm_ref,
    upd_ref, nf_ref, ns_ref, nst_ref, q_ref,
    gs, ms, us, gr, bs, bb, covs, rs, ss, gc, rf, af, ro, sums_a, sums_b, lin,
    g_s, g_r, m_s, m_r, u_s, u_r, b_s, b_r, c_s, c_r, a_s, a_r, x_s, x_r, y_s, y_r, own_sem,
):
    me = lax.axis_index("fsdp")
    core = lax.axis_index("basis")
    rp = gs.shape[1]
    rf_rows = bs.shape[1]
    kp = bs.shape[2]
    total = n * cols
    width = 384 if cols % 384 == 0 else cols
    fold = 8 * 128

    def chunk(ref, d):
        if split:
            return ref.at[d]
        return ref.at[:, pl.ds(pl.multiple_of(d * cols, 128), cols)]

    def peers(fn):
        def body(k, carry):
            fn(lax.rem(me + k, n))
            return carry
        lax.fori_loop(1, n, body, 0)

    def send(source_of, target, s_sem, r_sem):
        def one(d):
            pltpu.make_async_remote_copy(
                src_ref=source_of(d), dst_ref=target(me), send_sem=s_sem.at[d],
                recv_sem=r_sem.at[me], device_id={"fsdp": d}, device_id_type=MESH,
            ).start()
        peers(one)

    def wait_recv(source_of, target, s_sem, r_sem):
        def one(d):
            pltpu.make_async_remote_copy(
                src_ref=source_of(d), dst_ref=target(d), send_sem=s_sem.at[d],
                recv_sem=r_sem.at[d], device_id={"fsdp": d}, device_id_type=MESH,
            ).wait_recv()
        peers(one)

    def wait_send(source_of, target, s_sem, r_sem):
        def one(d):
            pltpu.make_async_remote_copy(
                src_ref=source_of(d), dst_ref=target(me), send_sem=s_sem.at[d],
                recv_sem=r_sem.at[me], device_id={"fsdp": d}, device_id_type=MESH,
            ).wait_send()
        peers(one)

    plane = 4 if n % 4 == 0 else 1
    mine = lax.rem(me, plane)
    base = me - mine

    def gather_copy(source, target, s_sem, r_sem, slot, d, s_at):
        return pltpu.make_async_remote_copy(
            src_ref=source, dst_ref=target(slot), send_sem=s_sem.at[s_at],
            recv_sem=r_sem.at[slot], device_id={"fsdp": d}, device_id_type=MESH,
        )

    def across(fn):
        def body(k, carry):
            fn(lax.rem(me + plane * k, n))
            return carry
        lax.fori_loop(1, n // plane, body, 0)

    def inside(fn):
        for k in range(1, plane):
            fn(base + lax.rem(mine + k, plane))

    def gather_start(source, target, s_sem, r_sem):
        def one(d):
            gather_copy(source, target, s_sem, r_sem, me, d, d).start()
        across(one)
        inside(one)

    def gather_forward(source, target, s_sem, r_sem):
        def one(z):
            gather_copy(source, target, s_sem, r_sem, z, z, z).wait_recv()

            def on(p):
                gather_copy(target(z), target, s_sem, r_sem, z, p, z - mine + p - base).start()

            inside(on)
        across(one)

    def gather_finish(source, target, s_sem, r_sem):
        def near(p):
            gather_copy(source, target, s_sem, r_sem, p, p, p).wait_recv()

            def far(z):
                slot = z - mine + p - base
                gather_copy(source, target, s_sem, r_sem, slot, p, slot).wait_recv()

            across(far)

        inside(near)

    def gather_sent(source, target, s_sem, r_sem):
        def one(d):
            gather_copy(source, target, s_sem, r_sem, d, d, d).wait_send()
        peers(one)

    grads = (lambda d: chunk(g_ref, d), lambda s: gs.at[s], g_s, g_r)
    moments = (lambda d: chunk(m_ref, d), lambda s: ms.at[s], m_s, m_r)
    updates = (lambda d: us.at[d], lambda s: chunk(upd_ref, s), u_s, u_r)
    bases = (eb_ref, lambda s: bs.at[s], b_s, b_r)
    shares = (lambda d: covs.at[d], lambda s: rs.at[s], c_s, c_r)
    stats = (nst_ref, lambda s: ss.at[s], a_s, a_r)
    squares = (lambda d: sums_a.at[n], lambda s: sums_a.at[s], x_s, x_r)

    barrier = pltpu.get_barrier_semaphore()

    def greet(d):
        pl.semaphore_signal(barrier, inc=1, device_id={"fsdp": d}, device_id_type=MESH)

    peers(greet)
    for k in range(1, nb):
        pl.semaphore_signal(
            barrier, inc=1, device_id={"basis": lax.rem(core + k, nb)}, device_id_type=MESH
        )
    pl.semaphore_wait(barrier, n - 1 + nb - 1)

    send(*grads)
    gather_start(*bases)
    own = [
        pltpu.make_async_copy(chunk(g_ref, me), gs.at[me], own_sem.at[0]),
        pltpu.make_async_copy(chunk(m_ref, me), ms.at[me], own_sem.at[1]),
        pltpu.make_async_copy(eb_ref, bs.at[me], own_sem.at[2]),
    ]
    for copy in own:
        copy.start()

    def add_squares(d, acc):
        v = chunk(g_ref, d)[...].astype(F32)
        return acc + jnp.sum(v * v, axis=0, keepdims=True)

    acc = lax.fori_loop(0, n, add_squares, jnp.zeros((1, cols), F32))
    sums_a[n] = jnp.full((8, 128), jnp.sum(acc), F32)
    send(*squares)
    sums_a[me] = sums_a[n]
    wait_recv(*squares)
    sums_b[nb] = jnp.sum(sums_a[0:n], axis=0)
    sums_b[core] = sums_b[nb]

    def cross(k):
        other = lax.rem(core + k, nb)
        return pltpu.make_async_remote_copy(
            src_ref=sums_b.at[nb], dst_ref=sums_b.at[core], send_sem=y_s.at[other],
            recv_sem=y_r.at[core], device_id={"basis": other}, device_id_type=MESH,
        )

    def cross_recv(k):
        other = lax.rem(core + k, nb)
        return pltpu.make_async_remote_copy(
            src_ref=sums_b.at[nb], dst_ref=sums_b.at[other], send_sem=y_s.at[other],
            recv_sem=y_r.at[other], device_id={"basis": other}, device_id_type=MESH,
        )

    for k in range(1, nb):
        cross(k).start()

    for copy in own:
        copy.wait()
    wait_recv(*grads)
    gc[...] = dot(pm_ref[...], gs[...].reshape(n * rp, cols), ((1,), (0,))).astype(BF16)

    def share(s, carry):
        covs[s] = dot(gs[s], gc[...], ((1,), (1,)))[:rf_rows]
        return carry

    lax.fori_loop(0, n, share, 0)
    send(*shares)
    gather_forward(*bases)

    for k in range(1, nb):
        cross_recv(k).wait_recv()
    mean = jnp.sum(sums_b[0:nb], axis=0)[0:1, 0:1] / entries
    clip = jnp.minimum(1.0, clip_rms / jnp.sqrt(mean + 1e-06))

    def first(d, carry):
        chunk(nf_ref, d)[...] = (
            beta_first * chunk(m_ref, d)[...].astype(F32)
            + (1.0 - beta_first) * clip * chunk(g_ref, d)[...].astype(F32)
        ).astype(BF16)
        return carry

    lax.fori_loop(0, n, first, 0)

    gather_finish(*bases)

    def narrow(s, carry):
        v = bs[s]
        if rp > rf_rows:
            v = jnp.concatenate([v, jnp.zeros((rp - rf_rows, kp), F32)], axis=0)
        bb[s] = v.astype(BF16)
        return carry

    lax.fori_loop(0, n, narrow, 0)

    def columns(i):
        if cols == width:
            return pl.ds(0, cols)
        return pl.ds(pl.multiple_of(i * width, 128), width)

    def rotate(i, carry):
        at = columns(i)
        basis = bb[...].reshape(n * rp, kp)[:, :bk]
        rot = clip * dot(basis, gs[:, :, at].reshape(n * rp, width), ((0,), (0,)))
        gr[:, at] = rot
        ns_ref[:, at] = (
            beta_second * v_ref[:, at].astype(F32) + (1.0 - beta_second) * rot * rot
        ).astype(BF16)
        return carry

    lax.fori_loop(0, cols // width, rotate, 0)

    wait_recv(*shares)
    rs[me] = covs[me]

    def add_share(s, acc):
        return acc + rs[s]

    cov = lax.fori_loop(0, n, add_share, jnp.zeros((rf_rows, kp), F32)) / total
    nst_ref[...] = beta_second * st_ref[...] + (1.0 - beta_second) * clip * clip * cov
    gather_start(*stats)
    ss[me] = nst_ref[...]
    gather_forward(*stats)
    gather_finish(*stats)
    send(*moments)

    def refresh(i, carry):
        at = pl.ds(pl.multiple_of(i * NB, NB), NB)
        rf[at, :] = dot(
            ss[:, :, at].reshape(n * rf_rows, NB), bs[...].reshape(n * rf_rows, kp),
            ((0,), (0,)), HI,
        )
        return carry

    lax.fori_loop(0, kp // NB, refresh, 0)
    rows = bk // n
    r_at = lax.broadcasted_iota(jnp.int32, (rf_rows, kp), 0)
    c_at = lax.broadcasted_iota(jnp.int32, (rf_rows, kp), 1)
    pick = jnp.where((c_at == r_at + me * rows) & (r_at < rows), 1.0, 0.0).astype(F32)
    ro[...] = dot(pick, rf[...], ((1,), (0,)), HI)

    def gram(i, carry):
        at = pl.ds(pl.multiple_of(i * NB, NB), NB)
        part = dot(rf[:, at], rf[...], ((0,), (0,)), HI)
        r = lax.broadcasted_iota(jnp.int32, (NB, kp), 0) + i * NB
        c = lax.broadcasted_iota(jnp.int32, (NB, kp), 1)
        af[at, :] = part + jnp.where((r == c) & (r >= bk), 1.0, 0.0)
        return carry

    lax.fori_loop(0, kp // NB, gram, 0)

    def precondition():
        wait_recv(*moments)

        def body(i, carry):
            at = columns(i)
            basis = bb[...].reshape(n * rp, kp)[:, :bk]
            rot = gr[:, at]
            moment = dot(basis, ms[:, :, at].reshape(n * rp, width), ((0,), (0,)))
            second = beta_second * v_ref[:, at].astype(F32) + (1.0 - beta_second) * rot * rot
            direction = (
                (beta_first * moment + (1.0 - beta_first) * rot) / (jnp.sqrt(second) + tiny_eps)
            ).astype(BF16)
            us[:, :, at] = (
                dot(basis, direction, ((1,), (0,))).astype(BF16).reshape(n, rp, width)
            )
            return carry

        lax.fori_loop(0, cols // width, body, 0)
        send(*updates)
        chunk(upd_ref, me)[...] = us[me]

    blocks = kp // NB

    def eliminate(b, steps):
        at = pl.ds(pl.multiple_of(b * NB, NB), NB)
        tiles = [
            af[pl.ds(pl.multiple_of(b * NB + 8 * t, 8), 8), at] for t in range(NB // 8)
        ]
        lin[...] = inverse_factor(tiles, steps)
        panel = dot(lin[...], af[at, :], ((1,), (0,)), HI)
        q = dot(ro[:, at], lin[...], ((1,), (1,)), HI)
        q_ref[:, at] = q
        ro[...] = ro[...] - dot(q, panel, ((1,), (0,)), HI)
        if steps == NB:
            af[...] = af[...] - dot(panel, panel, ((0,), (0,)), HI)

    def whole_block(b, carry):
        @pl.when(b == blocks // 2)
        def _():
            precondition()

        eliminate(b, NB)
        return carry

    last = bk - (blocks - 1) * NB
    lax.fori_loop(0, blocks - 1, whole_block, 0)
    eliminate(blocks - 1, last)

    wait_recv(*updates)
    for k in range(1, nb):
        cross(k).wait_send()
    for phase in (grads, squares, shares, moments, updates):
        wait_send(*phase)
    gather_sent(*bases)
    gather_sent(*stats)


def ceil_to(value, step):
    return -(-value // step) * step


def local(n, nb, gradient, first_moment, second_moment, statistic, eigenbasis):
    rows, ff = gradient.shape[1:]
    bk = rows * n
    cols = ff // n
    rp = ceil_to(rows, 16)
    rf_rows = ceil_to(rows, 8)
    kp = ceil_to(bk, NB)
    split = cols % 128 != 0

    def wide(x):
        x = jnp.pad(x[0], ((0, rp - rows), (0, 0)))
        if split:
            x = jnp.swapaxes(x.reshape(rp, n, cols), 0, 1)
        return x

    def narrow(x):
        if split:
            x = jnp.swapaxes(x, 0, 1).reshape(rp, ff)
        return x[None, :rows]

    def square(x):
        return jnp.pad(x[0], ((0, rf_rows - rows), (0, kp - bk)))

    pick = np.zeros((kp, n * rp), np.float32)
    at = np.arange(bk)
    pick[at, (at // rows) * rp + at % rows] = 1.0
    big = (n, rp, cols) if split else (rp, ff)
    vmem = pl.BlockSpec(memory_space=pltpu.VMEM)
    dma = pltpu.SemaphoreType.DMA
    upd, nf, ns, nst, q = pl.pallas_call(
        functools.partial(kernel, n, nb, nb * bk * ff, cols, bk, split),
        out_shape=(
            jax.ShapeDtypeStruct(big, BF16),
            jax.ShapeDtypeStruct(big, BF16),
            jax.ShapeDtypeStruct((bk, cols), BF16),
            jax.ShapeDtypeStruct((rf_rows, kp), F32),
            jax.ShapeDtypeStruct((rf_rows, kp), F32),
        ),
        in_specs=[vmem] * 6,
        out_specs=(vmem,) * 5,
        scratch_shapes=[
            pltpu.VMEM((n, rp, cols), BF16),
            pltpu.VMEM((n, rp, cols), BF16),
            pltpu.VMEM((n, rp, cols), BF16),
            pltpu.VMEM((bk, cols), F32),
            pltpu.VMEM((n, rf_rows, kp), F32),
            pltpu.VMEM((n, rp, kp), BF16),
            pltpu.VMEM((n, rf_rows, kp), F32),
            pltpu.VMEM((n, rf_rows, kp), F32),
            pltpu.VMEM((n, rf_rows, kp), F32),
            pltpu.VMEM((kp, cols), BF16),
            pltpu.VMEM((kp, kp), F32),
            pltpu.VMEM((kp, kp), F32),
            pltpu.VMEM((rf_rows, kp), F32),
            pltpu.VMEM((n + 1, 8, 128), F32),
            pltpu.VMEM((nb + 1, 8, 128), F32),
            pltpu.VMEM((NB, NB), F32),
        ]
        + [dma((n,))] * 14
        + [dma((nb,))] * 2
        + [dma((3,))],
        compiler_params=pltpu.CompilerParams(
            collective_id=0, has_side_effects=True, vmem_limit_bytes=56 * 1024 * 1024
        ),
    )(
        wide(gradient),
        wide(first_moment),
        second_moment[0],
        square(statistic),
        square(eigenbasis),
        jnp.asarray(pick, BF16),
    )
    return (narrow(upd), narrow(nf), ns[None], nst[None, :rows, :bk], q[None, :rows, :bk])


def solution(mesh):
    n, nb = mesh.shape["fsdp"], mesh.shape["basis"]
    rows = P("basis", "fsdp", None)
    columns = P("basis", None, "fsdp")
    return jax.shard_map(
        functools.partial(local, n, nb),
        mesh=mesh,
        in_specs=(rows, rows, columns, rows, rows),
        out_specs=(rows, rows, columns, rows, rows),
        check_vma=False,
    )
```

```python
import functools

import jax
import jax.numpy as jnp
import numpy as np
from jax import lax
from jax.experimental import pallas as pl
from jax.experimental.pallas import tpu as pltpu
from jax.sharding import PartitionSpec as P

beta_first = 0.9
beta_second = 0.95
clip_rms = 0.5
tiny_eps = 1e-08
NB = 128
MESH = pl.DeviceIdType.MESH
HI = lax.Precision.HIGHEST
F32 = jnp.float32
BF16 = jnp.bfloat16


def dot(left, right, dims, precision=None):
    return lax.dot_general(
        left, right, (dims, ((), ())), preferred_element_type=F32, precision=precision
    )


def inverse_factor(tiles, steps):
    lane = lax.broadcasted_iota(jnp.int32, (8, NB), 1)
    row = lax.broadcasted_iota(jnp.int32, (8, NB), 0)
    count = NB // 8
    active = -(-steps // 8)
    for j in range(0, steps, 2):
        home, sub = divmod(j, 8)
        here, after = lane == j, lane == j + 1
        one = tiles[home][sub : sub + 1, :]
        two = tiles[home][sub + 1 : sub + 2, :]
        cross = two[:, j : j + 1]
        inverse = 1.0 / one[:, j : j + 1]
        ratio = cross * inverse
        inverse_two = 1.0 / (two[:, j + 1 : j + 2] - cross * ratio)
        lead = jnp.where(here[:1], 1.0, jnp.where(after[:1], 0.0, one))
        trail = jnp.where(
            after[:1], 1.0, jnp.where(here[:1], 0.0, two) - ratio * lead
        )
        scaled_two = trail * inverse_two
        scaled_one = lead * inverse - ratio * scaled_two
        kept = jnp.where(after[:1], two - ratio * one, trail)
        for t in range(home, active):
            column = tiles[t][:, j : j + 1]
            column_two = tiles[t][:, j + 1 : j + 2]
            updated = (
                jnp.where(here | after, 0.0, tiles[t])
                - column * scaled_one - column_two * scaled_two
            )
            if t == home:
                updated = jnp.where(row > sub + 1, updated, tiles[t])
                updated = jnp.where(row == sub + 1, kept, updated)
            tiles[t] = updated
    out = []
    for t in range(count):
        on_diag = lane == row + 8 * t
        pivot = jnp.sum(jnp.where(on_diag, tiles[t], 0.0), axis=1, keepdims=True)
        unit = jnp.where(on_diag, 1.0, jnp.where(lane < row + 8 * t, tiles[t], 0.0))
        out.append(unit * lax.rsqrt(pivot))
    return jnp.concatenate(out, axis=0)


def kernel(
    n, nb, entries, cols, bk, split,
    g_ref, m_ref, v_ref, st_ref, eb_ref, pm_ref,
    upd_ref, nf_ref, ns_ref, nst_ref, q_ref,
    gs, ms, us, gr, bs, bb, covs, rs, ss, gc, rf, af, ro, sums_a, sums_b, lin, rt, f_s, f_r,
    g_s, g_r, m_s, m_r, u_s, u_r, b_s, b_r, c_s, c_r, a_s, a_r, x_s, x_r, y_s, y_r, own_sem,
):
    me = lax.axis_index("fsdp")
    core = lax.axis_index("basis")
    rp = gs.shape[1]
    rf_rows = bs.shape[1]
    kp = bs.shape[2]
    total = n * cols
    width = 384 if cols % 384 == 0 else cols
    fold = 8 * 128

    def chunk(ref, d):
        if split:
            return ref.at[d]
        return ref.at[:, pl.ds(pl.multiple_of(d * cols, 128), cols)]

    def peers(fn):
        def body(k, carry):
            fn(lax.rem(me + k, n))
            return carry
        lax.fori_loop(1, n, body, 0)

    def send(source_of, target, s_sem, r_sem):
        def one(d):
            pltpu.make_async_remote_copy(
                src_ref=source_of(d), dst_ref=target(me), send_sem=s_sem.at[d],
                recv_sem=r_sem.at[me], device_id={"fsdp": d}, device_id_type=MESH,
            ).start()
        peers(one)

    def wait_recv(source_of, target, s_sem, r_sem):
        def one(d):
            pltpu.make_async_remote_copy(
                src_ref=source_of(d), dst_ref=target(d), send_sem=s_sem.at[d],
                recv_sem=r_sem.at[d], device_id={"fsdp": d}, device_id_type=MESH,
            ).wait_recv()
        peers(one)

    def wait_send(source_of, target, s_sem, r_sem):
        def one(d):
            pltpu.make_async_remote_copy(
                src_ref=source_of(d), dst_ref=target(me), send_sem=s_sem.at[d],
                recv_sem=r_sem.at[me], device_id={"fsdp": d}, device_id_type=MESH,
            ).wait_send()
        peers(one)

    plane = 4 if n % 4 == 0 else 1
    mine = lax.rem(me, plane)
    base = me - mine

    def gather_copy(source, target, s_sem, r_sem, slot, d, s_at):
        return pltpu.make_async_remote_copy(
            src_ref=source, dst_ref=target(slot), send_sem=s_sem.at[s_at],
            recv_sem=r_sem.at[slot], device_id={"fsdp": d}, device_id_type=MESH,
        )

    def across(fn):
        def body(k, carry):
            fn(lax.rem(me + plane * k, n))
            return carry
        lax.fori_loop(1, n // plane, body, 0)

    def inside(fn):
        for k in range(1, plane):
            fn(base + lax.rem(mine + k, plane))

    def gather_start(source, target, s_sem, r_sem):
        def one(d):
            gather_copy(source, target, s_sem, r_sem, me, d, d).start()
        across(one)
        inside(one)

    def gather_forward(source, target, s_sem, r_sem):
        def one(z):
            gather_copy(source, target, s_sem, r_sem, z, z, z).wait_recv()

            def on(p):
                gather_copy(target(z), target, s_sem, r_sem, z, p, z - mine + p - base).start()

            inside(on)
        across(one)

    def gather_finish(source, target, s_sem, r_sem):
        def near(p):
            gather_copy(source, target, s_sem, r_sem, p, p, p).wait_recv()

            def far(z):
                slot = z - mine + p - base
                gather_copy(source, target, s_sem, r_sem, slot, p, slot).wait_recv()

            across(far)

        inside(near)

    def gather_sent(source, target, s_sem, r_sem):
        def one(d):
            gather_copy(source, target, s_sem, r_sem, d, d, d).wait_send()
        peers(one)

    grads = (lambda d: chunk(g_ref, d), lambda s: gs.at[s], g_s, g_r)
    moments = (lambda d: chunk(m_ref, d), lambda s: ms.at[s], m_s, m_r)
    updates = (lambda d: us.at[d], lambda s: chunk(upd_ref, s), u_s, u_r)
    bases = (eb_ref, lambda s: bs.at[s], b_s, b_r)
    stats = (nst_ref, lambda s: ss.at[s], a_s, a_r)
    squares = (lambda d: sums_a.at[n], lambda s: sums_a.at[s], x_s, x_r)

    barrier = pltpu.get_barrier_semaphore()

    def greet(d):
        pl.semaphore_signal(barrier, inc=1, device_id={"fsdp": d}, device_id_type=MESH)

    peers(greet)
    for k in range(1, nb):
        pl.semaphore_signal(
            barrier, inc=1, device_id={"basis": lax.rem(core + k, nb)}, device_id_type=MESH
        )
    pl.semaphore_wait(barrier, n - 1 + nb - 1)

    send(*grads)
    gather_start(*bases)
    own = [
        pltpu.make_async_copy(chunk(g_ref, me), gs.at[me], own_sem.at[0]),
        pltpu.make_async_copy(chunk(m_ref, me), ms.at[me], own_sem.at[1]),
        pltpu.make_async_copy(eb_ref, bs.at[me], own_sem.at[2]),
    ]
    for copy in own:
        copy.start()

    def add_squares(d, acc):
        v = chunk(g_ref, d)[...].astype(F32)
        return acc + jnp.sum(v * v, axis=0, keepdims=True)

    acc = lax.fori_loop(0, n, add_squares, jnp.zeros((1, cols), F32))
    sums_a[n] = jnp.full((8, 128), jnp.sum(acc), F32)
    send(*squares)
    sums_a[me] = sums_a[n]
    wait_recv(*squares)
    sums_b[nb] = jnp.sum(sums_a[0:n], axis=0)
    sums_b[core] = sums_b[nb]

    def cross(k):
        other = lax.rem(core + k, nb)
        return pltpu.make_async_remote_copy(
            src_ref=sums_b.at[nb], dst_ref=sums_b.at[core], send_sem=y_s.at[other],
            recv_sem=y_r.at[core], device_id={"basis": other}, device_id_type=MESH,
        )

    def cross_recv(k):
        other = lax.rem(core + k, nb)
        return pltpu.make_async_remote_copy(
            src_ref=sums_b.at[nb], dst_ref=sums_b.at[other], send_sem=y_s.at[other],
            recv_sem=y_r.at[other], device_id={"basis": other}, device_id_type=MESH,
        )

    for k in range(1, nb):
        cross(k).start()

    for copy in own:
        copy.wait()
    wait_recv(*grads)
    gc[...] = dot(pm_ref[...], gs[...].reshape(n * rp, cols), ((1,), (0,))).astype(BF16)

    def share(s, carry):
        covs[s] = dot(gs[s], gc[...], ((1,), (1,)))[:rf_rows]
        return carry

    lax.fori_loop(0, n, share, 0)
    per = n // plane

    def near_copy(p, k, slot, sem):
        return pltpu.make_async_remote_copy(
            src_ref=covs.at[slot], dst_ref=rs.at[sem], send_sem=c_s.at[slot],
            recv_sem=c_r.at[sem], device_id={"fsdp": p}, device_id_type=MESH,
        )

    def each_near(fn):
        def on(p):
            def body(k, carry):
                fn(p, k)
                return carry
            lax.fori_loop(0, per, body, 0)
        inside(on)

    def far_copy(z, slot):
        return pltpu.make_async_remote_copy(
            src_ref=covs.at[z], dst_ref=rt.at[slot], send_sem=f_s.at[z],
            recv_sem=f_r.at[slot], device_id={"fsdp": z}, device_id_type=MESH,
        )

    each_near(lambda p, k: near_copy(p, k, k * plane + p - base, mine * per + k).start())
    gather_forward(*bases)
    send(*moments)

    for k in range(1, nb):
        cross_recv(k).wait_recv()
    mean = jnp.sum(sums_b[0:nb], axis=0)[0:1, 0:1] / entries
    clip = jnp.minimum(1.0, clip_rms / jnp.sqrt(mean + 1e-06))

    def first(d, carry):
        chunk(nf_ref, d)[...] = (
            beta_first * chunk(m_ref, d)[...].astype(F32)
            + (1.0 - beta_first) * clip * chunk(g_ref, d)[...].astype(F32)
        ).astype(BF16)
        return carry

    lax.fori_loop(0, n, first, 0)

    gather_finish(*bases)

    def narrow(s, carry):
        v = bs[s]
        if rp > rf_rows:
            v = jnp.concatenate([v, jnp.zeros((rp - rf_rows, kp), F32)], axis=0)
        bb[s] = v.astype(BF16)
        return carry

    lax.fori_loop(0, n, narrow, 0)

    def columns(i):
        if cols == width:
            return pl.ds(0, cols)
        return pl.ds(pl.multiple_of(i * width, 128), width)

    def rotate(i, carry):
        at = columns(i)
        basis = bb[...].reshape(n * rp, kp)[:, :bk]
        rot = clip * dot(basis, gs[:, :, at].reshape(n * rp, width), ((0,), (0,)))
        gr[:, at] = rot
        ns_ref[:, at] = (
            beta_second * v_ref[:, at].astype(F32) + (1.0 - beta_second) * rot * rot
        ).astype(BF16)
        return carry

    lax.fori_loop(0, cols // width, rotate, 0)

    each_near(
        lambda p, k: near_copy(p, k, k * plane + p - base, (p - base) * per + k).wait_recv()
    )
    level = base // plane

    def plane_sum(z):
        k = (z - mine) // plane
        acc = covs[z]
        for step in range(1, plane):
            acc = acc + rs[lax.rem(mine + step, plane) * per + k]
        return acc

    def pass_on(z):
        covs[z] = plane_sum(z)
        far_copy(z, level).start()

    across(pass_on)
    rt[level] = plane_sum(me)
    across(lambda z: far_copy(z, (z - mine) // plane).wait_recv())

    def add_share(k, acc):
        return acc + rt[k]

    cov = lax.fori_loop(0, per, add_share, jnp.zeros((rf_rows, kp), F32)) / total
    nst_ref[...] = beta_second * st_ref[...] + (1.0 - beta_second) * clip * clip * cov
    gather_start(*stats)
    ss[me] = nst_ref[...]
    gather_forward(*stats)
    gather_finish(*stats)

    def refresh(i, carry):
        at = pl.ds(pl.multiple_of(i * NB, NB), NB)
        rf[at, :] = dot(
            ss[:, :, at].reshape(n * rf_rows, NB), bs[...].reshape(n * rf_rows, kp),
            ((0,), (0,)), HI,
        )
        return carry

    lax.fori_loop(0, kp // NB, refresh, 0)
    rows = bk // n
    r_at = lax.broadcasted_iota(jnp.int32, (rf_rows, kp), 0)
    c_at = lax.broadcasted_iota(jnp.int32, (rf_rows, kp), 1)
    pick = jnp.where((c_at == r_at + me * rows) & (r_at < rows), 1.0, 0.0).astype(F32)
    ro[...] = dot(pick, rf[...], ((1,), (0,)), HI)

    def gram(i, carry):
        at = pl.ds(pl.multiple_of(i * NB, NB), NB)
        part = dot(rf[:, at], rf[...], ((0,), (0,)), HI)
        r = lax.broadcasted_iota(jnp.int32, (NB, kp), 0) + i * NB
        c = lax.broadcasted_iota(jnp.int32, (NB, kp), 1)
        af[at, :] = part + jnp.where((r == c) & (r >= bk), 1.0, 0.0)
        return carry

    lax.fori_loop(0, kp // NB, gram, 0)

    def precondition():
        wait_recv(*moments)

        def body(i, carry):
            at = columns(i)
            basis = bb[...].reshape(n * rp, kp)[:, :bk]
            rot = gr[:, at]
            moment = dot(basis, ms[:, :, at].reshape(n * rp, width), ((0,), (0,)))
            second = beta_second * v_ref[:, at].astype(F32) + (1.0 - beta_second) * rot * rot
            direction = (
                (beta_first * moment + (1.0 - beta_first) * rot) / (jnp.sqrt(second) + tiny_eps)
            ).astype(BF16)
            us[:, :, at] = (
                dot(basis, direction, ((1,), (0,))).astype(BF16).reshape(n, rp, width)
            )
            return carry

        lax.fori_loop(0, cols // width, body, 0)
        send(*updates)
        chunk(upd_ref, me)[...] = us[me]

    blocks = kp // NB

    def eliminate(b, steps):
        at = pl.ds(pl.multiple_of(b * NB, NB), NB)
        tiles = [
            af[pl.ds(pl.multiple_of(b * NB + 8 * t, 8), 8), at] for t in range(NB // 8)
        ]
        lin[...] = inverse_factor(tiles, steps)
        panel = dot(lin[...], af[at, :], ((1,), (0,)), HI)
        q = dot(ro[:, at], lin[...], ((1,), (1,)), HI)
        q_ref[:, at] = q
        ro[...] = ro[...] - dot(q, panel, ((1,), (0,)), HI)
        if steps == NB:
            af[...] = af[...] - dot(panel, panel, ((0,), (0,)), HI)

    def whole_block(b, carry):
        @pl.when(b == 1)
        def _():
            precondition()

        eliminate(b, NB)
        return carry

    last = bk - (blocks - 1) * NB
    lax.fori_loop(0, blocks - 1, whole_block, 0)
    eliminate(blocks - 1, last)

    wait_recv(*updates)
    for k in range(1, nb):
        cross(k).wait_send()
    for phase in (grads, squares, moments, updates):
        wait_send(*phase)
    each_near(lambda p, k: near_copy(p, k, k * plane + p - base, mine * per + k).wait_send())
    across(lambda z: far_copy(z, level).wait_send())
    gather_sent(*bases)
    gather_sent(*stats)


def ceil_to(value, step):
    return -(-value // step) * step


def local(n, nb, gradient, first_moment, second_moment, statistic, eigenbasis):
    rows, ff = gradient.shape[1:]
    bk = rows * n
    cols = ff // n
    rp = ceil_to(rows, 16)
    rf_rows = ceil_to(rows, 8)
    kp = ceil_to(bk, NB)
    split = cols % 128 != 0

    def wide(x):
        x = jnp.pad(x[0], ((0, rp - rows), (0, 0)))
        if split:
            x = jnp.swapaxes(x.reshape(rp, n, cols), 0, 1)
        return x

    def narrow(x):
        if split:
            x = jnp.swapaxes(x, 0, 1).reshape(rp, ff)
        return x[None, :rows]

    def square(x):
        return jnp.pad(x[0], ((0, rf_rows - rows), (0, kp - bk)))

    pick = np.zeros((kp, n * rp), np.float32)
    at = np.arange(bk)
    pick[at, (at // rows) * rp + at % rows] = 1.0
    big = (n, rp, cols) if split else (rp, ff)
    vmem = pl.BlockSpec(memory_space=pltpu.VMEM)
    dma = pltpu.SemaphoreType.DMA
    upd, nf, ns, nst, q = pl.pallas_call(
        functools.partial(kernel, n, nb, nb * bk * ff, cols, bk, split),
        out_shape=(
            jax.ShapeDtypeStruct(big, BF16),
            jax.ShapeDtypeStruct(big, BF16),
            jax.ShapeDtypeStruct((bk, cols), BF16),
            jax.ShapeDtypeStruct((rf_rows, kp), F32),
            jax.ShapeDtypeStruct((rf_rows, kp), F32),
        ),
        in_specs=[vmem] * 6,
        out_specs=(vmem,) * 5,
        scratch_shapes=[
            pltpu.VMEM((n, rp, cols), BF16),
            pltpu.VMEM((n, rp, cols), BF16),
            pltpu.VMEM((n, rp, cols), BF16),
            pltpu.VMEM((bk, cols), F32),
            pltpu.VMEM((n, rf_rows, kp), F32),
            pltpu.VMEM((n, rp, kp), BF16),
            pltpu.VMEM((n, rf_rows, kp), F32),
            pltpu.VMEM((n, rf_rows, kp), F32),
            pltpu.VMEM((n, rf_rows, kp), F32),
            pltpu.VMEM((kp, cols), BF16),
            pltpu.VMEM((kp, kp), F32),
            pltpu.VMEM((kp, kp), F32),
            pltpu.VMEM((rf_rows, kp), F32),
            pltpu.VMEM((n + 1, 8, 128), F32),
            pltpu.VMEM((nb + 1, 8, 128), F32),
            pltpu.VMEM((NB, NB), F32),
            pltpu.VMEM((n, rf_rows, kp), F32),
        ]
        + [dma((n,))] * 16
        + [dma((nb,))] * 2
        + [dma((3,))],
        compiler_params=pltpu.CompilerParams(
            collective_id=0, has_side_effects=True, vmem_limit_bytes=56 * 1024 * 1024
        ),
    )(
        wide(gradient),
        wide(first_moment),
        second_moment[0],
        square(statistic),
        square(eigenbasis),
        jnp.asarray(pick, BF16),
    )
    return (narrow(upd), narrow(nf), ns[None], nst[None, :rows, :bk], q[None, :rows, :bk])


def solution(mesh):
    n, nb = mesh.shape["fsdp"], mesh.shape["basis"]
    rows = P("basis", "fsdp", None)
    columns = P("basis", None, "fsdp")
    return jax.shard_map(
        functools.partial(local, n, nb),
        mesh=mesh,
        in_specs=(rows, rows, columns, rows, rows),
        out_specs=(rows, rows, columns, rows, rows),
        check_vma=False,
    )
```

```python
import functools

import jax
import jax.numpy as jnp
import numpy as np
from jax import lax
from jax.experimental import pallas as pl
from jax.experimental.pallas import tpu as pltpu
from jax.sharding import PartitionSpec as P

beta_first = 0.9
beta_second = 0.95
clip_rms = 0.5
tiny_eps = 1e-08
NB = 128
MESH = pl.DeviceIdType.MESH
HI = lax.Precision.HIGHEST
F32 = jnp.float32
BF16 = jnp.bfloat16


def dot(left, right, dims, precision=None):
    return lax.dot_general(
        left, right, (dims, ((), ())), preferred_element_type=F32, precision=precision
    )


def inverse_factor(tiles, steps):
    lane = lax.broadcasted_iota(jnp.int32, (8, NB), 1)
    row = lax.broadcasted_iota(jnp.int32, (8, NB), 0)
    count = NB // 8
    active = -(-steps // 8)
    for j in range(0, steps, 2):
        home, sub = divmod(j, 8)
        here, after = lane == j, lane == j + 1
        one = tiles[home][sub : sub + 1, :]
        two = tiles[home][sub + 1 : sub + 2, :]
        cross = two[:, j : j + 1]
        inverse = 1.0 / one[:, j : j + 1]
        ratio = cross * inverse
        inverse_two = 1.0 / (two[:, j + 1 : j + 2] - cross * ratio)
        lead = jnp.where(here[:1], 1.0, jnp.where(after[:1], 0.0, one))
        trail = jnp.where(
            after[:1], 1.0, jnp.where(here[:1], 0.0, two) - ratio * lead
        )
        scaled_two = trail * inverse_two
        scaled_one = lead * inverse - ratio * scaled_two
        kept = jnp.where(after[:1], two - ratio * one, trail)
        for t in range(home, active):
            column = tiles[t][:, j : j + 1]
            column_two = tiles[t][:, j + 1 : j + 2]
            updated = (
                jnp.where(here | after, 0.0, tiles[t])
                - column * scaled_one - column_two * scaled_two
            )
            if t == home:
                updated = jnp.where(row > sub + 1, updated, tiles[t])
                updated = jnp.where(row == sub + 1, kept, updated)
            tiles[t] = updated
    out = []
    for t in range(count):
        on_diag = lane == row + 8 * t
        pivot = jnp.sum(jnp.where(on_diag, tiles[t], 0.0), axis=1, keepdims=True)
        unit = jnp.where(on_diag, 1.0, jnp.where(lane < row + 8 * t, tiles[t], 0.0))
        out.append(unit * lax.rsqrt(pivot))
    return jnp.concatenate(out, axis=0)


def kernel(
    n, nb, entries, cols, bk, split,
    g_ref, m_ref, v_ref, st_ref, eb_ref, pm_ref,
    upd_ref, nf_ref, ns_ref, nst_ref, q_ref,
    gs, ms, us, gr, bs, bb, covs, rs, ss, gc, rf, af, ro, sums_a, sums_b, lin, rt, f_s, f_r,
    g_s, g_r, m_s, m_r, u_s, u_r, b_s, b_r, c_s, c_r, a_s, a_r, x_s, x_r, y_s, y_r, own_sem,
):
    me = lax.axis_index("fsdp")
    core = lax.axis_index("basis")
    rp = gs.shape[1]
    rf_rows = bs.shape[1]
    kp = bs.shape[2]
    total = n * cols
    width = 384 if cols % 384 == 0 else cols
    fold = 8 * 128

    def chunk(ref, d):
        if split:
            return ref.at[d]
        return ref.at[:, pl.ds(pl.multiple_of(d * cols, 128), cols)]

    def peers(fn):
        def body(k, carry):
            fn(lax.rem(me + k, n))
            return carry
        lax.fori_loop(1, n, body, 0)

    def send(source_of, target, s_sem, r_sem):
        def one(d):
            pltpu.make_async_remote_copy(
                src_ref=source_of(d), dst_ref=target(me), send_sem=s_sem.at[d],
                recv_sem=r_sem.at[me], device_id={"fsdp": d}, device_id_type=MESH,
            ).start()
        peers(one)

    def wait_recv(source_of, target, s_sem, r_sem):
        def one(d):
            pltpu.make_async_remote_copy(
                src_ref=source_of(d), dst_ref=target(d), send_sem=s_sem.at[d],
                recv_sem=r_sem.at[d], device_id={"fsdp": d}, device_id_type=MESH,
            ).wait_recv()
        peers(one)

    def wait_send(source_of, target, s_sem, r_sem):
        def one(d):
            pltpu.make_async_remote_copy(
                src_ref=source_of(d), dst_ref=target(me), send_sem=s_sem.at[d],
                recv_sem=r_sem.at[me], device_id={"fsdp": d}, device_id_type=MESH,
            ).wait_send()
        peers(one)

    plane = 4 if n % 4 == 0 else 1
    mine = lax.rem(me, plane)
    base = me - mine

    def gather_copy(source, target, s_sem, r_sem, slot, d, s_at):
        return pltpu.make_async_remote_copy(
            src_ref=source, dst_ref=target(slot), send_sem=s_sem.at[s_at],
            recv_sem=r_sem.at[slot], device_id={"fsdp": d}, device_id_type=MESH,
        )

    def across(fn):
        def body(k, carry):
            fn(lax.rem(me + plane * k, n))
            return carry
        lax.fori_loop(1, n // plane, body, 0)

    def inside(fn):
        for k in range(1, plane):
            fn(base + lax.rem(mine + k, plane))

    def gather_start(source, target, s_sem, r_sem):
        def one(d):
            gather_copy(source, target, s_sem, r_sem, me, d, d).start()
        across(one)
        inside(one)

    def gather_forward(source, target, s_sem, r_sem):
        def one(z):
            gather_copy(source, target, s_sem, r_sem, z, z, z).wait_recv()

            def on(p):
                gather_copy(target(z), target, s_sem, r_sem, z, p, z - mine + p - base).start()

            inside(on)
        across(one)

    def gather_finish(source, target, s_sem, r_sem):
        def near(p):
            gather_copy(source, target, s_sem, r_sem, p, p, p).wait_recv()

            def far(z):
                slot = z - mine + p - base
                gather_copy(source, target, s_sem, r_sem, slot, p, slot).wait_recv()

            across(far)

        inside(near)

    def gather_sent(source, target, s_sem, r_sem):
        def one(d):
            gather_copy(source, target, s_sem, r_sem, d, d, d).wait_send()
        peers(one)

    grads = (lambda d: chunk(g_ref, d), lambda s: gs.at[s], g_s, g_r)
    moments = (lambda d: chunk(m_ref, d), lambda s: ms.at[s], m_s, m_r)
    updates = (lambda d: us.at[d], lambda s: chunk(upd_ref, s), u_s, u_r)
    bases = (eb_ref, lambda s: bs.at[s], b_s, b_r)
    stats = (nst_ref, lambda s: ss.at[s], a_s, a_r)
    squares = (lambda d: sums_a.at[n], lambda s: sums_a.at[s], x_s, x_r)

    barrier = pltpu.get_barrier_semaphore()

    def greet(d):
        pl.semaphore_signal(barrier, inc=1, device_id={"fsdp": d}, device_id_type=MESH)

    peers(greet)
    for k in range(1, nb):
        pl.semaphore_signal(
            barrier, inc=1, device_id={"basis": lax.rem(core + k, nb)}, device_id_type=MESH
        )
    pl.semaphore_wait(barrier, n - 1 + nb - 1)

    send(*grads)
    gather_start(*bases)
    own = [
        pltpu.make_async_copy(chunk(g_ref, me), gs.at[me], own_sem.at[0]),
        pltpu.make_async_copy(chunk(m_ref, me), ms.at[me], own_sem.at[1]),
        pltpu.make_async_copy(eb_ref, bs.at[me], own_sem.at[2]),
    ]
    for copy in own:
        copy.start()

    def add_squares(d, acc):
        v = chunk(g_ref, d)[...].astype(F32)
        return acc + jnp.sum(v * v, axis=0, keepdims=True)

    acc = lax.fori_loop(0, n, add_squares, jnp.zeros((1, cols), F32))
    sums_a[n] = jnp.full((8, 128), jnp.sum(acc), F32)
    send(*squares)
    sums_a[me] = sums_a[n]
    wait_recv(*squares)
    sums_b[nb] = jnp.sum(sums_a[0:n], axis=0)
    sums_b[core] = sums_b[nb]

    def cross(k):
        other = lax.rem(core + k, nb)
        return pltpu.make_async_remote_copy(
            src_ref=sums_b.at[nb], dst_ref=sums_b.at[core], send_sem=y_s.at[other],
            recv_sem=y_r.at[core], device_id={"basis": other}, device_id_type=MESH,
        )

    def cross_recv(k):
        other = lax.rem(core + k, nb)
        return pltpu.make_async_remote_copy(
            src_ref=sums_b.at[nb], dst_ref=sums_b.at[other], send_sem=y_s.at[other],
            recv_sem=y_r.at[other], device_id={"basis": other}, device_id_type=MESH,
        )

    for k in range(1, nb):
        cross(k).start()

    for copy in own:
        copy.wait()
    wait_recv(*grads)
    gc[...] = dot(pm_ref[...], gs[...].reshape(n * rp, cols), ((1,), (0,))).astype(BF16)

    def share(s, carry):
        covs[s] = dot(gs[s], gc[...], ((1,), (1,)))[:rf_rows]
        return carry

    lax.fori_loop(0, n, share, 0)
    per = n // plane

    def near_copy(p, k, slot, sem):
        return pltpu.make_async_remote_copy(
            src_ref=covs.at[slot], dst_ref=rs.at[sem], send_sem=c_s.at[slot],
            recv_sem=c_r.at[sem], device_id={"fsdp": p}, device_id_type=MESH,
        )

    def each_near(fn):
        def on(p):
            def body(k, carry):
                fn(p, k)
                return carry
            lax.fori_loop(0, per, body, 0)
        inside(on)

    def far_copy(z, slot):
        return pltpu.make_async_remote_copy(
            src_ref=covs.at[z], dst_ref=rt.at[slot], send_sem=f_s.at[z],
            recv_sem=f_r.at[slot], device_id={"fsdp": z}, device_id_type=MESH,
        )

    each_near(lambda p, k: near_copy(p, k, k * plane + p - base, mine * per + k).start())
    gather_forward(*bases)

    for k in range(1, nb):
        cross_recv(k).wait_recv()
    mean = jnp.sum(sums_b[0:nb], axis=0)[0:1, 0:1] / entries
    clip = jnp.minimum(1.0, clip_rms / jnp.sqrt(mean + 1e-06))

    def first(d, carry):
        chunk(nf_ref, d)[...] = (
            beta_first * chunk(m_ref, d)[...].astype(F32)
            + (1.0 - beta_first) * clip * chunk(g_ref, d)[...].astype(F32)
        ).astype(BF16)
        return carry

    lax.fori_loop(0, n, first, 0)

    gather_finish(*bases)

    def narrow(s, carry):
        v = bs[s]
        if rp > rf_rows:
            v = jnp.concatenate([v, jnp.zeros((rp - rf_rows, kp), F32)], axis=0)
        bb[s] = v.astype(BF16)
        return carry

    lax.fori_loop(0, n, narrow, 0)

    def columns(i):
        if cols == width:
            return pl.ds(0, cols)
        return pl.ds(pl.multiple_of(i * width, 128), width)

    def rotate(i, carry):
        at = columns(i)
        basis = bb[...].reshape(n * rp, kp)[:, :bk]
        rot = clip * dot(basis, gs[:, :, at].reshape(n * rp, width), ((0,), (0,)))
        gr[:, at] = rot
        ns_ref[:, at] = (
            beta_second * v_ref[:, at].astype(F32) + (1.0 - beta_second) * rot * rot
        ).astype(BF16)
        return carry

    lax.fori_loop(0, cols // width, rotate, 0)

    each_near(
        lambda p, k: near_copy(p, k, k * plane + p - base, (p - base) * per + k).wait_recv()
    )
    level = base // plane

    def plane_sum(z):
        k = (z - mine) // plane
        acc = covs[z]
        for step in range(1, plane):
            acc = acc + rs[lax.rem(mine + step, plane) * per + k]
        return acc

    def pass_on(z):
        covs[z] = plane_sum(z)
        far_copy(z, level).start()

    across(pass_on)
    rt[level] = plane_sum(me)
    across(lambda z: far_copy(z, (z - mine) // plane).wait_recv())

    def add_share(k, acc):
        return acc + rt[k]

    cov = lax.fori_loop(0, per, add_share, jnp.zeros((rf_rows, kp), F32)) / total
    nst_ref[...] = beta_second * st_ref[...] + (1.0 - beta_second) * clip * clip * cov
    gather_start(*stats)
    ss[me] = nst_ref[...]
    gather_forward(*stats)
    gather_finish(*stats)
    send(*moments)

    def refresh(i, carry):
        at = pl.ds(pl.multiple_of(i * NB, NB), NB)
        rf[at, :] = dot(
            ss[:, :, at].reshape(n * rf_rows, NB), bs[...].reshape(n * rf_rows, kp),
            ((0,), (0,)), HI,
        )
        return carry

    lax.fori_loop(0, kp // NB, refresh, 0)
    rows = bk // n
    r_at = lax.broadcasted_iota(jnp.int32, (rf_rows, kp), 0)
    c_at = lax.broadcasted_iota(jnp.int32, (rf_rows, kp), 1)
    pick = jnp.where((c_at == r_at + me * rows) & (r_at < rows), 1.0, 0.0).astype(F32)
    ro[...] = dot(pick, rf[...], ((1,), (0,)), HI)

    def gram(i, carry):
        at = pl.ds(pl.multiple_of(i * NB, NB), NB)
        part = dot(rf[:, at], rf[...], ((0,), (0,)), HI)
        r = lax.broadcasted_iota(jnp.int32, (NB, kp), 0) + i * NB
        c = lax.broadcasted_iota(jnp.int32, (NB, kp), 1)
        af[at, :] = part + jnp.where((r == c) & (r >= bk), 1.0, 0.0)
        return carry

    lax.fori_loop(0, kp // NB, gram, 0)

    def precondition():
        wait_recv(*moments)

        def body(i, carry):
            at = columns(i)
            basis = bb[...].reshape(n * rp, kp)[:, :bk]
            rot = gr[:, at]
            moment = dot(basis, ms[:, :, at].reshape(n * rp, width), ((0,), (0,)))
            second = beta_second * v_ref[:, at].astype(F32) + (1.0 - beta_second) * rot * rot
            direction = (
                (beta_first * moment + (1.0 - beta_first) * rot) / (jnp.sqrt(second) + tiny_eps)
            ).astype(BF16)
            us[:, :, at] = (
                dot(basis, direction, ((1,), (0,))).astype(BF16).reshape(n, rp, width)
            )
            return carry

        lax.fori_loop(0, cols // width, body, 0)
        send(*updates)
        chunk(upd_ref, me)[...] = us[me]

    blocks = kp // NB

    def eliminate(b, steps):
        at = pl.ds(pl.multiple_of(b * NB, NB), NB)
        tiles = [
            af[pl.ds(pl.multiple_of(b * NB + 8 * t, 8), 8), at] for t in range(NB // 8)
        ]
        lin[...] = inverse_factor(tiles, steps)
        panel = dot(lin[...], af[at, :], ((1,), (0,)), HI)
        q = dot(ro[:, at], lin[...], ((1,), (1,)), HI)
        q_ref[:, at] = q
        ro[...] = ro[...] - dot(q, panel, ((1,), (0,)), HI)
        if steps == NB:
            af[...] = af[...] - dot(panel, panel, ((0,), (0,)), HI)

    def whole_block(b, carry):
        @pl.when(b == blocks // 2)
        def _():
            precondition()

        eliminate(b, NB)
        return carry

    last = bk - (blocks - 1) * NB
    lax.fori_loop(0, blocks - 1, whole_block, 0)
    eliminate(blocks - 1, last)

    wait_recv(*updates)
    for k in range(1, nb):
        cross(k).wait_send()
    for phase in (grads, squares, moments, updates):
        wait_send(*phase)
    each_near(lambda p, k: near_copy(p, k, k * plane + p - base, mine * per + k).wait_send())
    across(lambda z: far_copy(z, level).wait_send())
    gather_sent(*bases)
    gather_sent(*stats)


def ceil_to(value, step):
    return -(-value // step) * step


def local(n, nb, gradient, first_moment, second_moment, statistic, eigenbasis):
    rows, ff = gradient.shape[1:]
    bk = rows * n
    cols = ff // n
    rp = ceil_to(rows, 16)
    rf_rows = ceil_to(rows, 8)
    kp = ceil_to(bk, NB)
    split = cols % 128 != 0

    def wide(x):
        x = jnp.pad(x[0], ((0, rp - rows), (0, 0)))
        if split:
            x = jnp.swapaxes(x.reshape(rp, n, cols), 0, 1)
        return x

    def narrow(x):
        if split:
            x = jnp.swapaxes(x, 0, 1).reshape(rp, ff)
        return x[None, :rows]

    def square(x):
        return jnp.pad(x[0], ((0, rf_rows - rows), (0, kp - bk)))

    pick = np.zeros((kp, n * rp), np.float32)
    at = np.arange(bk)
    pick[at, (at // rows) * rp + at % rows] = 1.0
    big = (n, rp, cols) if split else (rp, ff)
    vmem = pl.BlockSpec(memory_space=pltpu.VMEM)
    dma = pltpu.SemaphoreType.DMA
    upd, nf, ns, nst, q = pl.pallas_call(
        functools.partial(kernel, n, nb, nb * bk * ff, cols, bk, split),
        out_shape=(
            jax.ShapeDtypeStruct(big, BF16),
            jax.ShapeDtypeStruct(big, BF16),
            jax.ShapeDtypeStruct((bk, cols), BF16),
            jax.ShapeDtypeStruct((rf_rows, kp), F32),
            jax.ShapeDtypeStruct((rf_rows, kp), F32),
        ),
        in_specs=[vmem] * 6,
        out_specs=(vmem,) * 5,
        scratch_shapes=[
            pltpu.VMEM((n, rp, cols), BF16),
            pltpu.VMEM((n, rp, cols), BF16),
            pltpu.VMEM((n, rp, cols), BF16),
            pltpu.VMEM((bk, cols), F32),
            pltpu.VMEM((n, rf_rows, kp), F32),
            pltpu.VMEM((n, rp, kp), BF16),
            pltpu.VMEM((n, rf_rows, kp), F32),
            pltpu.VMEM((n, rf_rows, kp), F32),
            pltpu.VMEM((n, rf_rows, kp), F32),
            pltpu.VMEM((kp, cols), BF16),
            pltpu.VMEM((kp, kp), F32),
            pltpu.VMEM((kp, kp), F32),
            pltpu.VMEM((rf_rows, kp), F32),
            pltpu.VMEM((n + 1, 8, 128), F32),
            pltpu.VMEM((nb + 1, 8, 128), F32),
            pltpu.VMEM((NB, NB), F32),
            pltpu.VMEM((n, rf_rows, kp), F32),
        ]
        + [dma((n,))] * 16
        + [dma((nb,))] * 2
        + [dma((3,))],
        compiler_params=pltpu.CompilerParams(
            collective_id=0, has_side_effects=True, vmem_limit_bytes=56 * 1024 * 1024
        ),
    )(
        wide(gradient),
        wide(first_moment),
        second_moment[0],
        square(statistic),
        square(eigenbasis),
        jnp.asarray(pick, BF16),
    )
    return (narrow(upd), narrow(nf), ns[None], nst[None, :rows, :bk], q[None, :rows, :bk])


def solution(mesh):
    n, nb = mesh.shape["fsdp"], mesh.shape["basis"]
    rows = P("basis", "fsdp", None)
    columns = P("basis", None, "fsdp")
    return jax.shard_map(
        functools.partial(local, n, nb),
        mesh=mesh,
        in_specs=(rows, rows, columns, rows, rows),
        out_specs=(rows, rows, columns, rows, rows),
        check_vma=False,
    )
```
